32 devices in a mesh: grp: 2 (over y), gx: 4 (over x, core), gy: 4 (over z).
Axes of the slice: x: 2, y: 2, z: 4, core: 2. Of those that a mesh axis runs over, the one named last changes fastest.
Arguments:
- tokens: bfloat16 [2048, 18432], P(('grp', 'gy'), 'gx'), parts along dimension 0, may hold values from -6 to 6
- gate_weight: bfloat16 [18432, 9216], P('gx', ('grp', 'gy')), parts along dimension 1, may hold values from -0.046875 to 0.046875
- up_weight: bfloat16 [18432, 9216], P('gx', ('grp', 'gy')), parts along dimension 1, may hold values from -0.046875 to 0.046875
- down_weight: bfloat16 [9216, 18432], P(('grp', 'gy'), 'gx'), parts along dimension 0, may hold values from -0.09375 to 0.09375
Outputs:
- mixed: bfloat16 [2048, 18432], P(('grp', 'gy'), 'gx'), parts along dimension 0
The draws below stay inside these ranges and needn't reach their ends.
There are 2 independent parts, one for each index of `grp`. The reference program is written for one: setup_inputs(seed, part) draws one part's arguments, and reference() takes and returns one part's arrays. A program takes and returns all parts, laid end to end along the dimension named above; each array names one. Nothing has to cross between parts.
All inputs are finite; a program needn't handle non-finite values.
Results may differ from the reference program's by a relative error of at most 0.02.
Values may be sent and summed in bfloat16 or wider, within the bound.
A program may use at most 128 MiB of HBM per device.

```python
import jax
import jax.numpy as jnp
from jax import lax

D = 18432
FF = 4608
TOKENS = 1024
N_GY = 4


def levels(rng, dims, cuts, least, largest):
    factor_of, own = 1.0, jax.random.fold_in(rng, 6)
    for axis_at, blocks in cuts:
        steps = jnp.exp(jax.random.uniform(jax.random.fold_in(own, axis_at), (blocks,), jnp.float32, least / len(cuts), largest / len(cuts)))
        factor_of = factor_of * jnp.repeat(steps, dims[axis_at] // blocks).reshape([-1 if axis == axis_at else 1 for axis in range(len(dims))])
    return factor_of


def normal_values(rng, dims, deviation, reach, split=(), kind=jnp.bfloat16):
    drawn = jax.random.normal(rng, dims, jnp.float32) * deviation
    if len(split) > 0:
        drawn = levels(rng, dims, split, -0.22, 0.18) * drawn
    return jnp.clip(drawn, min=-reach, max=reach).astype(kind)


def setup_inputs(seed: int = 0, part: int = 0) -> dict:
    streams_of = jax.random.split(jax.random.key(seed), 5)
    part_keys = jax.random.split(jax.random.fold_in(streams_of[4], part), 5)
    tokens = normal_values(part_keys[0], (TOKENS, D), 1.0, 6.0, ((0, 4), (1, 4)))
    gate_weight = normal_values(part_keys[1], (D, FF), D ** -0.5, 0.046875, ((0, 4), (1, 4)))
    up_weight = normal_values(part_keys[2], (D, FF), D ** -0.5, 0.046875, ((0, 4), (1, 4)))
    down_weight = normal_values(part_keys[3], (FF, D), FF ** -0.5, 0.09375, ((0, 4), (1, 4)))
    return dict(tokens=tokens, gate_weight=gate_weight, up_weight=up_weight, down_weight=down_weight)


def reference(tokens, gate_weight, up_weight, down_weight):
    gate = jnp.dot(tokens, gate_weight, preferred_element_type=jnp.float32)
    up_vals = jnp.dot(tokens, up_weight, preferred_element_type=jnp.float32)
    hidden = (jax.nn.silu(gate) * up_vals).astype(jnp.bfloat16)
    units = FF // N_GY
    total = jnp.zeros((TOKENS, D), jnp.float32)
    for block in range(N_GY):
        partial_sum = jnp.dot(hidden[:, block * units:(block + 1) * units], down_weight[block * units:(block + 1) * units, :], preferred_element_type=jnp.float32)
        rounded = lax.optimization_barrier(partial_sum.astype(jnp.bfloat16))
        total = total + rounded.astype(jnp.float32)
    return total.astype(jnp.bfloat16)
```

```python
import functools

import jax
import jax.numpy as jnp
from jax import lax
from jax.experimental import pallas as pl
from jax.experimental.pallas import tpu as pltpu
from jax.sharding import PartitionSpec as P

MESH = pl.DeviceIdType.MESH
CHUNKS = 8
TILE = 256
F32 = jnp.float32
BF16 = jnp.bfloat16


def fused(
    n_gx, n_gy, chunks,
    tok, wg, wu, wd, out,
    w_in, w_down, xg, sums, gu, gu_in, hid,
    w_sem, own_sem, out_sem,
    ag_send, ag_recv, rs_send, rs_recv, gu_send, gu_recv, h_send, h_recv,
):
    x = lax.axis_index("gx")
    z = lax.axis_index("gy")
    last = n_gy - 1
    rows = xg.shape[2]
    width = xg.shape[3]
    units = hid.shape[2]
    part = hid.shape[1]
    total = n_gy * rows

    def peer(o):
        return lax.rem(x + o, n_gx)

    barrier = pltpu.get_barrier_semaphore()
    for o in range(1, n_gx):
        pl.semaphore_signal(barrier, inc=1, device_id={"gx": peer(o)}, device_id_type=MESH)

    @pl.when(z > 0)
    def _():
        pl.semaphore_signal(barrier, inc=1, device_id={"gy": z - 1}, device_id_type=MESH)

    @pl.when(z < last)
    def _():
        pl.semaphore_signal(barrier, inc=1, device_id={"gy": z + 1}, device_id_type=MESH)

    def own_copy(c):
        return pltpu.make_async_copy(tok.at[pl.ds(c * rows, rows)], xg.at[c, z], own_sem.at[c])

    loads = [
        pltpu.make_async_copy(wg, w_in.at[:, pl.ds(0, units)], w_sem.at[0]),
        pltpu.make_async_copy(wu, w_in.at[:, pl.ds(units, units)], w_sem.at[1]),
        pltpu.make_async_copy(wd, w_down, w_sem.at[2]),
    ]

    pl.semaphore_wait(barrier, n_gx - 1 + jnp.where(z > 0, 1, 0) + jnp.where(z < last, 1, 0))

    def ag_copy(c, q, to, own):
        q_sem = jnp.where(to < z, n_gy, q) if own else q
        src = tok.at[pl.ds(c * rows, rows)] if own else xg.at[c, q]
        return pltpu.make_async_remote_copy(
            src_ref=src, dst_ref=xg.at[c, q],
            send_sem=ag_send.at[c, q_sem], recv_sem=ag_recv.at[c, q],
            device_id={"gy": to}, device_id_type=MESH,
        )

    def ag_first(c):
        @pl.when(z < last)
        def _():
            ag_copy(c, z, z + 1, True).start()

        @pl.when(z > 0)
        def _():
            ag_copy(c, z, z - 1, True).start()

    def ag_step(c, s):
        @pl.when(z - s >= 0)
        def _():
            q = z - s
            ag_copy(c, q, z - 1, False).wait_recv()

            @pl.when(z < last)
            def _():
                ag_copy(c, q, z + 1, False).start()

        @pl.when(z + s <= last)
        def _():
            q = z + s
            ag_copy(c, q, z + 1, False).wait_recv()

            @pl.when(z > 0)
            def _():
                ag_copy(c, q, z - 1, False).start()

    def ag_sent(c):
        @pl.when(z < last)
        def _():
            ag_copy(c, z, z + 1, True).wait_send()

        @pl.when(z > 0)
        def _():
            ag_copy(c, z, z - 1, True).wait_send()

        for s in range(1, n_gy):
            @pl.when((z - s >= 0) & (z < last))
            def _():
                ag_copy(c, z - s, z + 1, False).wait_send()

            @pl.when((z + s <= last) & (z > 0))
            def _():
                ag_copy(c, z + s, z - 1, False).wait_send()

    def gu_copy(o):
        return pltpu.make_async_remote_copy(
            src_ref=gu.at[peer(o)], dst_ref=gu_in.at[o - 1],
            send_sem=gu_send.at[o - 1], recv_sem=gu_recv.at[o - 1],
            device_id={"gx": peer(o)}, device_id_type=MESH,
        )

    def h_copy(o):
        return pltpu.make_async_remote_copy(
            src_ref=hid.at[x], dst_ref=hid.at[x],
            send_sem=h_send.at[o - 1], recv_sem=h_recv.at[o - 1],
            device_id={"gx": peer(o)}, device_id_type=MESH,
        )

    def gate_up(c):
        own_copy(c).wait()

        @pl.when(c == 0)
        def _():
            loads[0].wait()
            loads[1].wait()

        @pl.loop(0, 2 * units // TILE)
        def _(i):
            cols = pl.ds(pl.multiple_of(i * TILE, TILE), TILE)
            prod = jnp.dot(
                xg[c].reshape(total, width), w_in[:, cols], preferred_element_type=F32
            )
            gu[:, :, cols] = prod.astype(BF16).reshape(n_gx, part, TILE)

        for o in range(1, n_gx):
            gu_copy(o).start()

    def hidden(c):
        for o in range(1, n_gx):
            gu_copy(o).wait_recv()

        @pl.loop(0, units // 128)
        def _(i):
            a = pl.ds(pl.multiple_of(i * 128, 128), 128)
            b = pl.ds(pl.multiple_of(units + i * 128, 128), 128)
            gate = gu[x, :, a].astype(F32)
            up = gu[x, :, b].astype(F32)
            for o in range(n_gx - 1):
                gate += gu_in[o, :, a].astype(F32)
                up += gu_in[o, :, b].astype(F32)
            hid[x, :, a] = (gate / (1.0 + jnp.exp(-gate)) * up).astype(BF16)

        for o in range(1, n_gx):
            h_copy(o).start()
        for o in range(1, n_gx):
            gu_copy(o).wait_send()

    def down(c):
        @pl.when(c == 0)
        def _():
            loads[2].wait()

        ag_sent(c)
        for o in range(1, n_gx):
            h_copy(o).wait_recv()

        @pl.loop(0, width // TILE)
        def _(i):
            cols = pl.ds(pl.multiple_of(i * TILE, TILE), TILE)
            prod = jnp.dot(
                hid[...].reshape(total, units), w_down[:, cols], preferred_element_type=F32
            )
            xg[c, :, :, cols] = prod.astype(BF16).reshape(n_gy, rows, TILE)

        for o in range(1, n_gx):
            h_copy(o).wait_send()

    def rs_copy(c, d, to):
        slot = jnp.where((to < z) & (d == to), n_gy, d)
        return pltpu.make_async_remote_copy(
            src_ref=xg.at[c, d], dst_ref=sums.at[c, slot],
            send_sem=rs_send.at[c, d], recv_sem=rs_recv.at[c, slot],
            device_id={"gy": to}, device_id_type=MESH,
        )

    def rs_arrived(c, slot, frm):
        pltpu.make_async_remote_copy(
            src_ref=xg.at[c, 0], dst_ref=sums.at[c, slot],
            send_sem=rs_send.at[c, 0], recv_sem=rs_recv.at[c, slot],
            device_id={"gy": frm}, device_id_type=MESH,
        ).wait_recv()

    def add(c, d, slots):
        step = 512 if width % 512 == 0 else 128

        @pl.loop(0, width // step)
        def _(i):
            cols = pl.ds(pl.multiple_of(i * step, step), step)
            acc = xg[c, d, :, cols].astype(F32)
            for slot in slots:
                acc += sums[c, slot, :, cols].astype(F32)
            xg[c, d, :, cols] = acc.astype(BF16)

    def rs_step(c, t):
        @pl.when((z <= t) & (z < last))
        def _():
            d = last - (t - z)

            @pl.when(z > 0)
            def _():
                rs_arrived(c, d, z - 1)
                add(c, d, [d])

            rs_copy(c, d, z + 1).start()

        @pl.when((last - z <= t) & (z > 0))
        def _():
            d = t - (last - z)

            @pl.when(z < last)
            def _():
                rs_arrived(c, d, z + 1)
                add(c, d, [d])

            rs_copy(c, d, z - 1).start()

    def out_copy(c):
        return pltpu.make_async_copy(xg.at[c, z], out.at[pl.ds(c * rows, rows)], out_sem.at[c])

    def rs_last(c):
        @pl.when(z > 0)
        def _():
            rs_arrived(c, z, z - 1)

        @pl.when(z < last)
        def _():
            rs_arrived(c, n_gy, z + 1)

        @pl.when((z > 0) & (z < last))
        def _():
            add(c, z, [z, n_gy])

        @pl.when(z == 0)
        def _():
            add(c, z, [n_gy])

        @pl.when(z == last)
        def _():
            add(c, z, [z])

        out_copy(c).start()

    def finish(c):
        out_copy(c).wait()
        for d in range(n_gy):
            @pl.when(d > z)
            def _():
                rs_copy(c, d, z + 1).wait_send()

            @pl.when(d < z)
            def _():
                rs_copy(c, d, z - 1).wait_send()

    ag_first(0)
    own_copy(0).start()
    for load in loads:
        load.start()
    for c in range(1, chunks):
        own_copy(c).start()

    @pl.loop(0, chunks + 2)
    def _(p):
        def when(c, f, *args):
            @pl.when((c >= 0) & (c < chunks))
            def _():
                f(c, *args)

        when(p - 1, gate_up)
        when(p, ag_step, 1)
        when(p - 2, rs_step, 1)
        when(p - 1, hidden)
        for s in range(2, last):
            when(p, ag_step, s)
            if s == 2:
                when(p + 1, ag_first)
            when(p - 2, rs_step, s)
        when(p - 1, down)
        when(p - 1, rs_step, 0)
        when(p, ag_step, last)
        when(p - 2, rs_last)

    @pl.loop(0, chunks)
    def _(c):
        finish(c)


def on_device_fused(n_gx, n_gy, tokens, gate_weight, up_weight, down_weight):
    held, width = tokens.shape
    units = gate_weight.shape[1]
    chunks = CHUNKS
    rows = held // chunks
    part = n_gy * rows // n_gx
    dma = pltpu.SemaphoreType.DMA
    return pl.pallas_call(
        functools.partial(fused, n_gx, n_gy, chunks),
        out_shape=jax.ShapeDtypeStruct((held, width), BF16),
        in_specs=[pl.BlockSpec(memory_space=pl.ANY)] * 4,
        out_specs=pl.BlockSpec(memory_space=pl.ANY),
        scratch_shapes=[
            pltpu.VMEM((width, 2 * units), BF16),
            pltpu.VMEM((units, width), BF16),
            pltpu.VMEM((chunks, n_gy, rows, width), BF16),
            pltpu.VMEM((chunks, n_gy + 1, rows, width), BF16),
            pltpu.VMEM((n_gx, part, 2 * units), BF16),
            pltpu.VMEM((n_gx - 1, part, 2 * units), BF16),
            pltpu.VMEM((n_gx, part, units), BF16),
            dma((3,)),
            dma((chunks,)),
            dma((chunks,)),
            dma((chunks, n_gy + 1)),
            dma((chunks, n_gy)),
            dma((chunks, n_gy)),
            dma((chunks, n_gy + 1)),
            dma((n_gx - 1,)),
            dma((n_gx - 1,)),
            dma((n_gx - 1,)),
            dma((n_gx - 1,)),
        ],
        compiler_params=pltpu.CompilerParams(
            collective_id=0, has_side_effects=True, vmem_limit_bytes=62 * 1024 * 1024
        ),
        cost_estimate=pl.CostEstimate(
            flops=6 * n_gy * held * width * units,
            bytes_accessed=2 * (3 * width * units + 2 * held * width),
            transcendentals=n_gy * held * units // n_gx,
        ),
    )(tokens, gate_weight, up_weight, down_weight)


def on_device_plain(tokens, gate_weight, up_weight, down_weight):
    units_dev = gate_weight.shape[1]
    w_both = jnp.concatenate([gate_weight, up_weight], axis=1)
    gathered = lax.all_gather(tokens, "gy", axis=0, tiled=True)
    shares = lax.psum_scatter(
        jnp.dot(gathered, w_both, preferred_element_type=F32).astype(BF16),
        "gx",
        scatter_dimension=0,
        tiled=True,
    ).astype(F32)
    hidden = (jax.nn.silu(shares[:, :units_dev]) * shares[:, units_dev:]).astype(BF16)
    hidden_all = lax.all_gather(hidden, "gx", axis=0, tiled=True)
    return lax.psum_scatter(
        jnp.dot(hidden_all, down_weight, preferred_element_type=F32).astype(BF16),
        "gy",
        scatter_dimension=0,
        tiled=True,
    )


def solution(mesh):
    n_gx, n_gy = mesh.shape["gx"], mesh.shape["gy"]
    in_specs = (
        P(("grp", "gy"), "gx"),
        P("gx", ("grp", "gy")),
        P("gx", ("grp", "gy")),
        P(("grp", "gy"), "gx"),
    )

    def on_device(tokens, gate_weight, up_weight, down_weight):
        held, width = tokens.shape
        units = gate_weight.shape[1]
        rows = held // CHUNKS
        fits = (
            held % (16 * CHUNKS) == 0
            and n_gy * rows % (16 * n_gx) == 0
            and units % 128 == 0
            and width % TILE == 0
            and n_gx > 1
            and n_gy > 3
        )
        if fits:
            return on_device_fused(n_gx, n_gy, tokens, gate_weight, up_weight, down_weight)
        return on_device_plain(tokens, gate_weight, up_weight, down_weight)

    return jax.shard_map(
        on_device,
        mesh=mesh,
        in_specs=in_specs,
        out_specs=P(("grp", "gy"), "gx"),
        check_vma=False,
    )
```

```python
import functools

import jax
import jax.numpy as jnp
from jax import lax
from jax.experimental import pallas as pl
from jax.experimental.pallas import tpu as pltpu
from jax.sharding import PartitionSpec as P

MESH = pl.DeviceIdType.MESH
CHUNKS = 8
TILE = 768
F32 = jnp.float32
BF16 = jnp.bfloat16


def fused(
    n_gx, n_gy, chunks,
    tok, wg, wu, wd, out,
    w_in, w_down, xg, sums, gu, gu_in, hid,
    w_sem, own_sem, out_sem,
    ag_send, ag_recv, rs_send, rs_recv, gu_send, gu_recv, h_send, h_recv,
):
    x = lax.axis_index("gx")
    z = lax.axis_index("gy")
    last = n_gy - 1
    rows = xg.shape[2]
    width = xg.shape[3]
    units = hid.shape[2]
    part = hid.shape[1]
    total = n_gy * rows

    def peer(o):
        return lax.rem(x + o, n_gx)

    barrier = pltpu.get_barrier_semaphore()
    for o in range(1, n_gx):
        pl.semaphore_signal(barrier, inc=1, device_id={"gx": peer(o)}, device_id_type=MESH)

    @pl.when(z > 0)
    def _():
        pl.semaphore_signal(barrier, inc=1, device_id={"gy": z - 1}, device_id_type=MESH)

    @pl.when(z < last)
    def _():
        pl.semaphore_signal(barrier, inc=1, device_id={"gy": z + 1}, device_id_type=MESH)

    def own_copy(c):
        return pltpu.make_async_copy(tok.at[pl.ds(c * rows, rows)], xg.at[c, z], own_sem.at[c])

    loads = [
        pltpu.make_async_copy(wg, w_in.at[:, pl.ds(0, units)], w_sem.at[0]),
        pltpu.make_async_copy(wu, w_in.at[:, pl.ds(units, units)], w_sem.at[1]),
        pltpu.make_async_copy(wd, w_down, w_sem.at[2]),
    ]

    pl.semaphore_wait(barrier, n_gx - 1 + jnp.where(z > 0, 1, 0) + jnp.where(z < last, 1, 0))

    def ag_copy(c, q, to, own):
        q_sem = jnp.where(to < z, n_gy, q) if own else q
        src = tok.at[pl.ds(c * rows, rows)] if own else xg.at[c, q]
        return pltpu.make_async_remote_copy(
            src_ref=src, dst_ref=xg.at[c, q],
            send_sem=ag_send.at[c, q_sem], recv_sem=ag_recv.at[c, q],
            device_id={"gy": to}, device_id_type=MESH,
        )

    def ag_first(c):
        @pl.when(z < last)
        def _():
            ag_copy(c, z, z + 1, True).start()

        @pl.when(z > 0)
        def _():
            ag_copy(c, z, z - 1, True).start()

    def ag_step(c, s):
        @pl.when(z - s >= 0)
        def _():
            q = z - s
            ag_copy(c, q, z - 1, False).wait_recv()

            @pl.when(z < last)
            def _():
                ag_copy(c, q, z + 1, False).start()

        @pl.when(z + s <= last)
        def _():
            q = z + s
            ag_copy(c, q, z + 1, False).wait_recv()

            @pl.when(z > 0)
            def _():
                ag_copy(c, q, z - 1, False).start()

    def ag_sent(c):
        @pl.when(z < last)
        def _():
            ag_copy(c, z, z + 1, True).wait_send()

        @pl.when(z > 0)
        def _():
            ag_copy(c, z, z - 1, True).wait_send()

        for s in range(1, n_gy):
            @pl.when((z - s >= 0) & (z < last))
            def _():
                ag_copy(c, z - s, z + 1, False).wait_send()

            @pl.when((z + s <= last) & (z > 0))
            def _():
                ag_copy(c, z + s, z - 1, False).wait_send()

    def gu_copy(o):
        return pltpu.make_async_remote_copy(
            src_ref=gu.at[peer(o)], dst_ref=gu_in.at[o - 1],
            send_sem=gu_send.at[o - 1], recv_sem=gu_recv.at[o - 1],
            device_id={"gx": peer(o)}, device_id_type=MESH,
        )

    def h_copy(o):
        return pltpu.make_async_remote_copy(
            src_ref=hid.at[x], dst_ref=hid.at[x],
            send_sem=h_send.at[o - 1], recv_sem=h_recv.at[o - 1],
            device_id={"gx": peer(o)}, device_id_type=MESH,
        )

    def gate_up(c):
        own_copy(c).wait()

        @pl.when(c == 0)
        def _():
            loads[0].wait()
            loads[1].wait()

        @pl.loop(0, 2 * units // TILE)
        def _(i):
            cols = pl.ds(pl.multiple_of(i * TILE, TILE), TILE)
            prod = jnp.dot(
                xg[c].reshape(total, width), w_in[:, cols], preferred_element_type=F32
            )
            gu[:, :, cols] = prod.astype(BF16).reshape(n_gx, part, TILE)

        for o in range(1, n_gx):
            gu_copy(o).start()

    def hidden(c):
        for o in range(1, n_gx):
            gu_copy(o).wait_recv()

        @pl.loop(0, units // 128)
        def _(i):
            a = pl.ds(pl.multiple_of(i * 128, 128), 128)
            b = pl.ds(pl.multiple_of(units + i * 128, 128), 128)
            gate = gu[x, :, a].astype(F32)
            up = gu[x, :, b].astype(F32)
            for o in range(n_gx - 1):
                gate += gu_in[o, :, a].astype(F32)
                up += gu_in[o, :, b].astype(F32)
            hid[x, :, a] = (gate / (1.0 + jnp.exp(-gate)) * up).astype(BF16)

        for o in range(1, n_gx):
            h_copy(o).start()
        for o in range(1, n_gx):
            gu_copy(o).wait_send()

    def down(c):
        @pl.when(c == 0)
        def _():
            loads[2].wait()

        ag_sent(c)
        for o in range(1, n_gx):
            h_copy(o).wait_recv()

        @pl.loop(0, width // TILE)
        def _(i):
            cols = pl.ds(pl.multiple_of(i * TILE, TILE), TILE)
            prod = jnp.dot(
                hid[...].reshape(total, units), w_down[:, cols], preferred_element_type=F32
            )
            xg[c, :, :, cols] = prod.astype(BF16).reshape(n_gy, rows, TILE)

        for o in range(1, n_gx):
            h_copy(o).wait_send()

    def rs_copy(c, d, to):
        slot = jnp.where((to < z) & (d == to), n_gy, d)
        return pltpu.make_async_remote_copy(
            src_ref=xg.at[c, d], dst_ref=sums.at[c, slot],
            send_sem=rs_send.at[c, d], recv_sem=rs_recv.at[c, slot],
            device_id={"gy": to}, device_id_type=MESH,
        )

    def rs_arrived(c, slot, frm):
        pltpu.make_async_remote_copy(
            src_ref=xg.at[c, 0], dst_ref=sums.at[c, slot],
            send_sem=rs_send.at[c, 0], recv_sem=rs_recv.at[c, slot],
            device_id={"gy": frm}, device_id_type=MESH,
        ).wait_recv()

    def add(c, d, slots):
        step = 512 if width % 512 == 0 else 128

        @pl.loop(0, width // step)
        def _(i):
            cols = pl.ds(pl.multiple_of(i * step, step), step)
            acc = xg[c, d, :, cols].astype(F32)
            for slot in slots:
                acc += sums[c, slot, :, cols].astype(F32)
            xg[c, d, :, cols] = acc.astype(BF16)

    def rs_step(c, t):
        @pl.when((z <= t) & (z < last))
        def _():
            d = last - (t - z)

            @pl.when(z > 0)
            def _():
                rs_arrived(c, d, z - 1)
                add(c, d, [d])

            rs_copy(c, d, z + 1).start()

        @pl.when((last - z <= t) & (z > 0))
        def _():
            d = t - (last - z)

            @pl.when(z < last)
            def _():
                rs_arrived(c, d, z + 1)
                add(c, d, [d])

            rs_copy(c, d, z - 1).start()

    def out_copy(c):
        return pltpu.make_async_copy(xg.at[c, z], out.at[pl.ds(c * rows, rows)], out_sem.at[c])

    def rs_last(c):
        @pl.when(z > 0)
        def _():
            rs_arrived(c, z, z - 1)

        @pl.when(z < last)
        def _():
            rs_arrived(c, n_gy, z + 1)

        @pl.when((z > 0) & (z < last))
        def _():
            add(c, z, [z, n_gy])

        @pl.when(z == 0)
        def _():
            add(c, z, [n_gy])

        @pl.when(z == last)
        def _():
            add(c, z, [z])

        out_copy(c).start()

    def finish(c):
        out_copy(c).wait()
        for d in range(n_gy):
            @pl.when(d > z)
            def _():
                rs_copy(c, d, z + 1).wait_send()

            @pl.when(d < z)
            def _():
                rs_copy(c, d, z - 1).wait_send()

    ag_first(0)
    own_copy(0).start()
    for load in loads:
        load.start()
    for c in range(1, chunks):
        own_copy(c).start()

    @pl.loop(0, chunks + 2)
    def _(p):
        def when(c, f, *args):
            @pl.when((c >= 0) & (c < chunks))
            def _():
                f(c, *args)

        when(p, ag_step, 1)
        when(p + 1, ag_first)
        when(p - 1, gate_up)
        when(p - 2, rs_step, 1)
        when(p, ag_step, 2)
        when(p - 1, hidden)
        when(p - 2, rs_step, 2)
        when(p, ag_step, 3)
        when(p - 1, down)
        when(p - 1, rs_step, 0)
        when(p - 2, rs_last)

    @pl.loop(0, chunks)
    def _(c):
        finish(c)


def on_device_fused(n_gx, n_gy, tokens, gate_weight, up_weight, down_weight):
    held, width = tokens.shape
    units = gate_weight.shape[1]
    chunks = CHUNKS
    rows = held // chunks
    part = n_gy * rows // n_gx
    dma = pltpu.SemaphoreType.DMA
    return pl.pallas_call(
        functools.partial(fused, n_gx, n_gy, chunks),
        out_shape=jax.ShapeDtypeStruct((held, width), BF16),
        in_specs=[pl.BlockSpec(memory_space=pl.ANY)] * 4,
        out_specs=pl.BlockSpec(memory_space=pl.ANY),
        scratch_shapes=[
            pltpu.VMEM((width, 2 * units), BF16),
            pltpu.VMEM((units, width), BF16),
            pltpu.VMEM((chunks, n_gy, rows, width), BF16),
            pltpu.VMEM((chunks, n_gy + 1, rows, width), BF16),
            pltpu.VMEM((n_gx, part, 2 * units), BF16),
            pltpu.VMEM((n_gx - 1, part, 2 * units), BF16),
            pltpu.VMEM((n_gx, part, units), BF16),
            dma((3,)),
            dma((chunks,)),
            dma((chunks,)),
            dma((chunks, n_gy + 1)),
            dma((chunks, n_gy)),
            dma((chunks, n_gy)),
            dma((chunks, n_gy + 1)),
            dma((n_gx - 1,)),
            dma((n_gx - 1,)),
            dma((n_gx - 1,)),
            dma((n_gx - 1,)),
        ],
        compiler_params=pltpu.CompilerParams(
            collective_id=0, has_side_effects=True, vmem_limit_bytes=62 * 1024 * 1024
        ),
        cost_estimate=pl.CostEstimate(
            flops=6 * n_gy * held * width * units,
            bytes_accessed=2 * (3 * width * units + 2 * held * width),
            transcendentals=n_gy * held * units // n_gx,
        ),
    )(tokens, gate_weight, up_weight, down_weight)


def on_device_plain(tokens, gate_weight, up_weight, down_weight):
    units_dev = gate_weight.shape[1]
    w_both = jnp.concatenate([gate_weight, up_weight], axis=1)
    gathered = lax.all_gather(tokens, "gy", axis=0, tiled=True)
    shares = lax.psum_scatter(
        jnp.dot(gathered, w_both, preferred_element_type=F32).astype(BF16),
        "gx",
        scatter_dimension=0,
        tiled=True,
    ).astype(F32)
    hidden = (jax.nn.silu(shares[:, :units_dev]) * shares[:, units_dev:]).astype(BF16)
    hidden_all = lax.all_gather(hidden, "gx", axis=0, tiled=True)
    return lax.psum_scatter(
        jnp.dot(hidden_all, down_weight, preferred_element_type=F32).astype(BF16),
        "gy",
        scatter_dimension=0,
        tiled=True,
    )


def solution(mesh):
    n_gx, n_gy = mesh.shape["gx"], mesh.shape["gy"]
    in_specs = (
        P(("grp", "gy"), "gx"),
        P("gx", ("grp", "gy")),
        P("gx", ("grp", "gy")),
        P(("grp", "gy"), "gx"),
    )

    def on_device(tokens, gate_weight, up_weight, down_weight):
        held, width = tokens.shape
        units = gate_weight.shape[1]
        rows = held // CHUNKS
        fits = (
            held % (16 * CHUNKS) == 0
            and n_gy * rows % (16 * n_gx) == 0
            and units % 128 == 0
            and width % TILE == 0
            and n_gx > 1
            and n_gy > 3
        )
        if fits:
            return on_device_fused(n_gx, n_gy, tokens, gate_weight, up_weight, down_weight)
        return on_device_plain(tokens, gate_weight, up_weight, down_weight)

    return jax.shard_map(
        on_device,
        mesh=mesh,
        in_specs=in_specs,
        out_specs=P(("grp", "gy"), "gx"),
        check_vma=False,
    )
```

```python
import functools

import jax
import jax.numpy as jnp
from jax import lax
from jax.experimental import pallas as pl
from jax.experimental.pallas import tpu as pltpu
from jax.sharding import PartitionSpec as P

MESH = pl.DeviceIdType.MESH
CHUNKS = 8
TILE = 1152
F32 = jnp.float32
BF16 = jnp.bfloat16


def fused(
    n_gx, n_gy, chunks,
    tok, wg, wu, wd, out,
    w_in, w_down, xg, sums, gu, gu_in, hid,
    w_sem, own_sem, out_sem,
    ag_send, ag_recv, rs_send, rs_recv, gu_send, gu_recv, h_send, h_recv,
):
    x = lax.axis_index("gx")
    z = lax.axis_index("gy")
    last = n_gy - 1
    rows = xg.shape[2]
    width = xg.shape[3]
    units = hid.shape[2]
    part = hid.shape[1]
    total = n_gy * rows

    def peer(o):
        return lax.rem(x + o, n_gx)

    barrier = pltpu.get_barrier_semaphore()
    for o in range(1, n_gx):
        pl.semaphore_signal(barrier, inc=1, device_id={"gx": peer(o)}, device_id_type=MESH)

    @pl.when(z > 0)
    def _():
        pl.semaphore_signal(barrier, inc=1, device_id={"gy": z - 1}, device_id_type=MESH)

    @pl.when(z < last)
    def _():
        pl.semaphore_signal(barrier, inc=1, device_id={"gy": z + 1}, device_id_type=MESH)

    def own_copy(c):
        return pltpu.make_async_copy(tok.at[pl.ds(c * rows, rows)], xg.at[c, z], own_sem.at[c])

    loads = [
        pltpu.make_async_copy(wg, w_in.at[:, pl.ds(0, units)], w_sem.at[0]),
        pltpu.make_async_copy(wu, w_in.at[:, pl.ds(units, units)], w_sem.at[1]),
        pltpu.make_async_copy(wd, w_down, w_sem.at[2]),
    ]

    pl.semaphore_wait(barrier, n_gx - 1 + jnp.where(z > 0, 1, 0) + jnp.where(z < last, 1, 0))

    def ag_copy(c, q, to, own):
        q_sem = jnp.where(to < z, n_gy, q) if own else q
        src = tok.at[pl.ds(c * rows, rows)] if own else xg.at[c, q]
        return pltpu.make_async_remote_copy(
            src_ref=src, dst_ref=xg.at[c, q],
            send_sem=ag_send.at[c, q_sem], recv_sem=ag_recv.at[c, q],
            device_id={"gy": to}, device_id_type=MESH,
        )

    def ag_first(c):
        @pl.when(z < last)
        def _():
            ag_copy(c, z, z + 1, True).start()

        @pl.when(z > 0)
        def _():
            ag_copy(c, z, z - 1, True).start()

    def ag_step(c, s):
        @pl.when(z - s >= 0)
        def _():
            q = z - s
            ag_copy(c, q, z - 1, False).wait_recv()

            @pl.when(z < last)
            def _():
                ag_copy(c, q, z + 1, False).start()

        @pl.when(z + s <= last)
        def _():
            q = z + s
            ag_copy(c, q, z + 1, False).wait_recv()

            @pl.when(z > 0)
            def _():
                ag_copy(c, q, z - 1, False).start()

    def ag_sent(c):
        @pl.when(z < last)
        def _():
            ag_copy(c, z, z + 1, True).wait_send()

        @pl.when(z > 0)
        def _():
            ag_copy(c, z, z - 1, True).wait_send()

        for s in range(1, n_gy):
            @pl.when((z - s >= 0) & (z < last))
            def _():
                ag_copy(c, z - s, z + 1, False).wait_send()

            @pl.when((z + s <= last) & (z > 0))
            def _():
                ag_copy(c, z + s, z - 1, False).wait_send()

    def gu_copy(o):
        return pltpu.make_async_remote_copy(
            src_ref=gu.at[peer(o)], dst_ref=gu_in.at[o - 1],
            send_sem=gu_send.at[o - 1], recv_sem=gu_recv.at[o - 1],
            device_id={"gx": peer(o)}, device_id_type=MESH,
        )

    def h_copy(o):
        return pltpu.make_async_remote_copy(
            src_ref=hid.at[x], dst_ref=hid.at[x],
            send_sem=h_send.at[o - 1], recv_sem=h_recv.at[o - 1],
            device_id={"gx": peer(o)}, device_id_type=MESH,
        )

    def gate_up(c):
        own_copy(c).wait()

        @pl.when(c == 0)
        def _():
            loads[0].wait()
            loads[1].wait()

        @pl.loop(0, 2 * units // TILE)
        def _(i):
            cols = pl.ds(pl.multiple_of(i * TILE, TILE), TILE)
            prod = jnp.dot(
                xg[c].reshape(total, width), w_in[:, cols], preferred_element_type=F32
            )
            gu[:, :, cols] = prod.astype(BF16).reshape(n_gx, part, TILE)

        for o in range(1, n_gx):
            gu_copy(o).start()

    def hidden(c):
        for o in range(1, n_gx):
            gu_copy(o).wait_recv()

        @pl.loop(0, units // 128)
        def _(i):
            a = pl.ds(pl.multiple_of(i * 128, 128), 128)
            b = pl.ds(pl.multiple_of(units + i * 128, 128), 128)
            gate = gu[x, :, a].astype(F32)
            up = gu[x, :, b].astype(F32)
            for o in range(n_gx - 1):
                gate += gu_in[o, :, a].astype(F32)
                up += gu_in[o, :, b].astype(F32)
            hid[x, :, a] = (gate / (1.0 + jnp.exp(-gate)) * up).astype(BF16)

        for o in range(1, n_gx):
            h_copy(o).start()
        for o in range(1, n_gx):
            gu_copy(o).wait_send()

    def down(c):
        @pl.when(c == 0)
        def _():
            loads[2].wait()

        ag_sent(c)
        for o in range(1, n_gx):
            h_copy(o).wait_recv()

        @pl.loop(0, width // TILE)
        def _(i):
            cols = pl.ds(pl.multiple_of(i * TILE, TILE), TILE)
            prod = jnp.dot(
                hid[...].reshape(total, units), w_down[:, cols], preferred_element_type=F32
            )
            xg[c, :, :, cols] = prod.astype(BF16).reshape(n_gy, rows, TILE)

        for o in range(1, n_gx):
            h_copy(o).wait_send()

    def rs_copy(c, d, to):
        slot = jnp.where((to < z) & (d == to), n_gy, d)
        return pltpu.make_async_remote_copy(
            src_ref=xg.at[c, d], dst_ref=sums.at[c, slot],
            send_sem=rs_send.at[c, d], recv_sem=rs_recv.at[c, slot],
            device_id={"gy": to}, device_id_type=MESH,
        )

    def rs_arrived(c, slot, frm):
        pltpu.make_async_remote_copy(
            src_ref=xg.at[c, 0], dst_ref=sums.at[c, slot],
            send_sem=rs_send.at[c, 0], recv_sem=rs_recv.at[c, slot],
            device_id={"gy": frm}, device_id_type=MESH,
        ).wait_recv()

    def add(c, d, slots):
        step = 512 if width % 512 == 0 else 128

        @pl.loop(0, width // step)
        def _(i):
            cols = pl.ds(pl.multiple_of(i * step, step), step)
            acc = xg[c, d, :, cols].astype(F32)
            for slot in slots:
                acc += sums[c, slot, :, cols].astype(F32)
            xg[c, d, :, cols] = acc.astype(BF16)

    def rs_step(c, t):
        @pl.when((z <= t) & (z < last))
        def _():
            d = last - (t - z)

            @pl.when(z > 0)
            def _():
                rs_arrived(c, d, z - 1)
                add(c, d, [d])

            rs_copy(c, d, z + 1).start()

        @pl.when((last - z <= t) & (z > 0))
        def _():
            d = t - (last - z)

            @pl.when(z < last)
            def _():
                rs_arrived(c, d, z + 1)
                add(c, d, [d])

            rs_copy(c, d, z - 1).start()

    def out_copy(c):
        return pltpu.make_async_copy(xg.at[c, z], out.at[pl.ds(c * rows, rows)], out_sem.at[c])

    def rs_last(c):
        @pl.when(z > 0)
        def _():
            rs_arrived(c, z, z - 1)

        @pl.when(z < last)
        def _():
            rs_arrived(c, n_gy, z + 1)

        @pl.when((z > 0) & (z < last))
        def _():
            add(c, z, [z, n_gy])

        @pl.when(z == 0)
        def _():
            add(c, z, [n_gy])

        @pl.when(z == last)
        def _():
            add(c, z, [z])

        out_copy(c).start()

    def finish(c):
        out_copy(c).wait()
        for d in range(n_gy):
            @pl.when(d > z)
            def _():
                rs_copy(c, d, z + 1).wait_send()

            @pl.when(d < z)
            def _():
                rs_copy(c, d, z - 1).wait_send()

    ag_first(0)
    own_copy(0).start()
    for load in loads:
        load.start()
    for c in range(1, chunks):
        own_copy(c).start()

    @pl.loop(0, chunks + 2)
    def _(p):
        def when(c, f, *args):
            @pl.when((c >= 0) & (c < chunks))
            def _():
                f(c, *args)

        when(p, ag_step, 1)
        when(p + 1, ag_first)
        when(p - 1, gate_up)
        when(p - 2, rs_step, 1)
        when(p, ag_step, 2)
        when(p - 1, hidden)
        when(p - 2, rs_step, 2)
        when(p, ag_step, 3)
        when(p - 1, down)
        when(p - 1, rs_step, 0)
        when(p - 2, rs_last)

    @pl.loop(0, chunks)
    def _(c):
        finish(c)


def on_device_fused(n_gx, n_gy, tokens, gate_weight, up_weight, down_weight):
    held, width = tokens.shape
    units = gate_weight.shape[1]
    chunks = CHUNKS
    rows = held // chunks
    part = n_gy * rows // n_gx
    dma = pltpu.SemaphoreType.DMA
    return pl.pallas_call(
        functools.partial(fused, n_gx, n_gy, chunks),
        out_shape=jax.ShapeDtypeStruct((held, width), BF16),
        in_specs=[pl.BlockSpec(memory_space=pl.ANY)] * 4,
        out_specs=pl.BlockSpec(memory_space=pl.ANY),
        scratch_shapes=[
            pltpu.VMEM((width, 2 * units), BF16),
            pltpu.VMEM((units, width), BF16),
            pltpu.VMEM((chunks, n_gy, rows, width), BF16),
            pltpu.VMEM((chunks, n_gy + 1, rows, width), BF16),
            pltpu.VMEM((n_gx, part, 2 * units), BF16),
            pltpu.VMEM((n_gx - 1, part, 2 * units), BF16),
            pltpu.VMEM((n_gx, part, units), BF16),
            dma((3,)),
            dma((chunks,)),
            dma((chunks,)),
            dma((chunks, n_gy + 1)),
            dma((chunks, n_gy)),
            dma((chunks, n_gy)),
            dma((chunks, n_gy + 1)),
            dma((n_gx - 1,)),
            dma((n_gx - 1,)),
            dma((n_gx - 1,)),
            dma((n_gx - 1,)),
        ],
        compiler_params=pltpu.CompilerParams(
            collective_id=0, has_side_effects=True, vmem_limit_bytes=62 * 1024 * 1024
        ),
        cost_estimate=pl.CostEstimate(
            flops=6 * n_gy * held * width * units,
            bytes_accessed=2 * (3 * width * units + 2 * held * width),
            transcendentals=n_gy * held * units // n_gx,
        ),
    )(tokens, gate_weight, up_weight, down_weight)


def on_device_plain(tokens, gate_weight, up_weight, down_weight):
    units_dev = gate_weight.shape[1]
    w_both = jnp.concatenate([gate_weight, up_weight], axis=1)
    gathered = lax.all_gather(tokens, "gy", axis=0, tiled=True)
    shares = lax.psum_scatter(
        jnp.dot(gathered, w_both, preferred_element_type=F32).astype(BF16),
        "gx",
        scatter_dimension=0,
        tiled=True,
    ).astype(F32)
    hidden = (jax.nn.silu(shares[:, :units_dev]) * shares[:, units_dev:]).astype(BF16)
    hidden_all = lax.all_gather(hidden, "gx", axis=0, tiled=True)
    return lax.psum_scatter(
        jnp.dot(hidden_all, down_weight, preferred_element_type=F32).astype(BF16),
        "gy",
        scatter_dimension=0,
        tiled=True,
    )


def solution(mesh):
    n_gx, n_gy = mesh.shape["gx"], mesh.shape["gy"]
    in_specs = (
        P(("grp", "gy"), "gx"),
        P("gx", ("grp", "gy")),
        P("gx", ("grp", "gy")),
        P(("grp", "gy"), "gx"),
    )

    def on_device(tokens, gate_weight, up_weight, down_weight):
        held, width = tokens.shape
        units = gate_weight.shape[1]
        rows = held // CHUNKS
        fits = (
            held % (16 * CHUNKS) == 0
            and n_gy * rows % (16 * n_gx) == 0
            and units % 128 == 0
            and width % TILE == 0
            and 2 * units % TILE == 0
            and n_gx > 1
            and n_gy > 3
        )
        if fits:
            return on_device_fused(n_gx, n_gy, tokens, gate_weight, up_weight, down_weight)
        return on_device_plain(tokens, gate_weight, up_weight, down_weight)

    return jax.shard_map(
        on_device,
        mesh=mesh,
        in_specs=in_specs,
        out_specs=P(("grp", "gy"), "gx"),
        check_vma=False,
    )
```
